128 devices in a mesh: tm: 16 (over z_lo, x, core), space: 8 (over z_hi, y).
Axes of the slice: x: 4, y: 4, z: 4 (z_hi: 2, z_lo: 2; z = z_hi * 2 + z_lo), core: 2. Of those that a mesh axis runs over, the one named last changes fastest.
Arguments:
- residual: float32 [2, 32, 3, 4, 512, 512], P(None, 'tm', None, None, 'space'), may hold values from -6 to 6
Outputs:
- correction: float32 [2, 32, 3, 4, 512, 512], P(None, 'tm', None, None, 'space')
The draws below stay inside these ranges and needn't reach their ends.
All inputs are finite; a program needn't handle non-finite values.
Results may differ from the reference program's by a relative error of at most 0.00021.
Values sent between devices are 32-bit elements; how exact they have to be, the bound alone decides.
A program may use at most 128 MiB of HBM per device.

```python
import math
import jax
import jax.numpy as jnp

NY = 512
NZ = 512
TS = 32
KX = 4


def level_of(stream_key, shape, shards, smallest, largest):
    loudness, own = 1.0, jax.random.fold_in(stream_key, 6)
    for dim, shards_of in shards:
        steps = jnp.exp(jax.random.uniform(jax.random.fold_in(own, dim), (shards_of,), jnp.float32, smallest / len(shards), largest / len(shards)))
        loudness = loudness * jnp.repeat(steps, shape[dim] // shards_of).reshape([-1 if axis == dim else 1 for axis in range(len(shape))])
    return loudness


def scatter_about(own_key, extent, width, bound, cuts=(), kind=jnp.bfloat16):
    entries = width * jax.random.normal(own_key, extent, jnp.float32)
    if cuts:
        entries = entries * level_of(own_key, extent, cuts, -0.22, 0.18)
    return jnp.clip(entries, -bound, bound).astype(kind)


def setup_inputs(seed: int = 0) -> dict:
    key_list = jax.random.split(jax.random.key(seed), 2)
    return {
        "residual": scatter_about(key_list[0], (2, TS, 3, KX, NY, NZ), 1.0, 6.0, ((1, 16), (4, 8)), jnp.float32),
    }


circ_alpha = 0.1
step_dt = 0.25
viscosity = 6e-5


def signed_modes(count, first, length):
    index = first + jnp.arange(count, dtype=jnp.int32)
    return jnp.where(index < length // 2, index, index - length).astype(jnp.float32)


def shifted_solve(field, freq, wave_x, wave_z, wave_y):
    real_part = field[0]
    imag_part = field[1]
    along_x = wave_x[None, :, None, None]
    along_z = wave_z[None, None, :, None]
    along_y = wave_y[None, None, None, :]
    waves = (along_x, along_y, along_z)
    square = along_x * along_x + along_y * along_y + along_z * along_z
    proj_real = (waves[0] * real_part[:, 0] + waves[1] * real_part[:, 1] + waves[2] * real_part[:, 2]) / square
    proj_imag = (waves[0] * imag_part[:, 0] + waves[1] * imag_part[:, 1] + waves[2] * imag_part[:, 2]) / square
    root = circ_alpha ** (1.0 / TS)
    angle = (2.0 * math.pi / TS) * freq
    den_real = (1.0 - root * jnp.cos(angle))[:, None, None, None] / step_dt + viscosity * square
    den_imag = (root * jnp.sin(angle))[:, None, None, None] / step_dt
    modulus = den_real * den_real + den_imag * den_imag
    reals = []
    imags = []
    for comp in range(3):
        free_real = real_part[:, comp] - waves[comp] * proj_real
        free_imag = imag_part[:, comp] - waves[comp] * proj_imag
        reals.append((free_real * den_real + free_imag * den_imag) / modulus)
        imags.append((free_imag * den_real - free_real * den_imag) / modulus)
    return jnp.stack([jnp.stack(reals, axis=1), jnp.stack(imags, axis=1)], axis=0)


def reference(residual):
    field = residual[0] + 1j * residual[1]
    field = jnp.fft.fft(field, axis=4, norm="ortho")
    field = jnp.fft.fft(field, axis=3, norm="ortho")
    times = jnp.arange(TS).astype(jnp.float32)
    weight = jnp.exp(math.log(circ_alpha) * times / TS)[:, None, None, None, None]
    field = jnp.fft.fft(field * weight, axis=0)
    field = jnp.swapaxes(field, 3, 4)
    stacked = jnp.stack([jnp.real(field), jnp.imag(field)], axis=0)
    wave_x = jnp.arange(1, KX + 1).astype(jnp.float32)
    solved = shifted_solve(stacked, times, wave_x, signed_modes(NZ, 0, NZ), signed_modes(NY, 0, NY))
    field = solved[0] + 1j * solved[1]
    field = jnp.fft.ifft(field, axis=0) / weight
    return jnp.stack([jnp.real(field), jnp.imag(field)], axis=0).astype(jnp.float32)
```

```python
import math

import jax
import jax.numpy as jnp
import ml_dtypes
import numpy as np
from jax import lax
from jax.experimental import pallas as pl
from jax.experimental.pallas import tpu as pltpu
from jax.sharding import PartitionSpec as P

NY = 512
NZ = 512
TS = 32
KX = 4
ALPHA = 0.1
DT = 0.25
NU = 6e-05

MESH = pl.DeviceIdType.MESH
F32 = jnp.float32
BF16 = jnp.bfloat16

STAGES = 8
ROWS = 32
SPACE = 8
GROUP = 8
PIECE = 16
AHEAD = 2
PEERS = ((0, 1), (1, 0), (3, 0), (2, 1), (1, 1), (2, 0), (3, 1))


def split_table(table):
    table = table.astype(np.float32)
    high = table.astype(ml_dtypes.bfloat16)
    low = (table - high.astype(np.float32)).astype(ml_dtypes.bfloat16)
    return high, low


def fourier(length):
    index = np.arange(length)
    angle = 2.0 * np.pi / length * (index[:, None] * index[None, :] % length)
    return np.cos(angle) / np.sqrt(length), np.sin(angle) / np.sqrt(length)


def z_tables():
    cosine, sine = fourier(NZ)
    both = np.concatenate([cosine, sine], axis=1)
    both = both.reshape(SPACE, 2, ROWS, 2 * NZ).transpose(1, 0, 2, 3)
    return split_table(both.reshape(2, SPACE * ROWS, 2 * NZ))


def y_tables():
    cosine, sine = fourier(NY)
    local = NY // SPACE
    from_re = np.concatenate([cosine, -sine], axis=1).reshape(SPACE, 1, local, 2 * NY)
    from_im = np.concatenate([sine, cosine], axis=1).reshape(SPACE, 1, local, 2 * NY)
    both = np.concatenate([from_re, from_im], axis=1)
    return split_table(both.reshape(2 * NY, 2 * NY))


def split_value(value):
    high = value.astype(BF16)
    return high, (value - high.astype(F32)).astype(BF16)


def kernel(
    r_ref, tzh_ref, tzl_ref, tyh_ref, tyl_ref, out_ref,
    xin, tzh, tzl, tyh, tyl, rh, rl, zbuf, recv, lh, ll, phi, bbuf, frecv, tot, zrecv, cbuf, crecv, ostage,
    in_sem, tab_sem, out_sem, zs_sem, zr_sem, fs_sem, fr_sem, es_sem, er_sem, bs_sem, br_sem,
):
    tm, space = lax.axis_index("tm"), lax.axis_index("space")
    z_lo, mine = tm // GROUP, tm % GROUP
    z_hi, y_pos = space // 4, space % 4
    partner = (1 - z_lo) * GROUP + mine

    def peer(d):
        dy, dz = PEERS[d]
        return ((z_hi + dz) % 2) * 4 + (y_pos + dy) % 4

    planes = [
        pltpu.make_async_copy(r_ref.at[:, :, :, x], xin.at[x], in_sem.at[x])
        for x in range(KX)
    ]
    tables = [
        pltpu.make_async_copy(src, dst, tab_sem.at[i])
        for i, (src, dst) in enumerate(
            ((tzh_ref, tzh), (tzl_ref, tzl), (tyh_ref, tyh), (tyl_ref, tyl))
        )
    ]
    planes[0].start()
    for table in tables:
        table.start()
    for plane in planes[1:]:
        plane.start()

    barrier = pltpu.get_barrier_semaphore()
    for d in range(7):
        pl.semaphore_signal(barrier, inc=1, device_id=(tm, peer(d)), device_id_type=MESH)
    for d in range(1, GROUP):
        other = z_lo * GROUP + (mine + d) % GROUP
        pl.semaphore_signal(barrier, inc=1, device_id=(other, space), device_id_type=MESH)
    pl.semaphore_signal(barrier, inc=1, device_id=(partner, space), device_id_type=MESH)

    def space_copy(t, d):
        return pltpu.make_async_remote_copy(
            src_ref=zbuf.at[t, peer(d)], dst_ref=recv.at[t, space],
            send_sem=zs_sem.at[t, d], recv_sem=zr_sem.at[t, space],
            device_id=(tm, peer(d)), device_id_type=MESH,
        )

    def space_arrival(t, d):
        return pltpu.make_async_remote_copy(
            src_ref=zbuf.at[t, peer(d)], dst_ref=recv.at[t, peer(d)],
            send_sem=zs_sem.at[t, d], recv_sem=zr_sem.at[t, peer(d)],
            device_id=(tm, peer(d)), device_id_type=MESH,
        )

    def group_copy(src, dst, ssem, rsem, t, d, arrival):
        other = (mine + d) % GROUP
        slot = other if arrival else mine
        return pltpu.make_async_remote_copy(
            src_ref=src.at[t, other], dst_ref=dst.at[t, slot],
            send_sem=ssem.at[t, d], recv_sem=rsem.at[t, slot],
            device_id=(z_lo * GROUP + other, space), device_id_type=MESH,
        )

    def forward_copy(t, d, arrival=False):
        return group_copy(bbuf, frecv, fs_sem, fr_sem, t, d, arrival)

    def back_copy(t, d, arrival=False):
        return group_copy(cbuf, crecv, bs_sem, br_sem, t, d, arrival)

    def total_copy(t):
        return pltpu.make_async_remote_copy(
            src_ref=tot.at[t], dst_ref=zrecv.at[t], send_sem=es_sem.at[t], recv_sem=er_sem.at[t],
            device_id=(partner, space), device_id_type=MESH,
        )

    def output_copy(t):
        return pltpu.make_async_copy(
            ostage.at[t], out_ref.at[:, :, :, t // 2, pl.ds((t % 2) * ROWS, ROWS)], out_sem.at[t]
        )

    def waves(t, first, count):
        row = lax.broadcasted_iota(jnp.int32, (count, NY), 0) + first
        col = lax.broadcasted_iota(jnp.int32, (count, NY), 1)
        wave_z = jnp.where(row < NZ // 2, row, row - NZ).astype(F32)
        wave_y = jnp.where(col < NY // 2, col, col - NY).astype(F32)
        wave_x = (t // 2 + 1).astype(F32)
        return wave_x, wave_y, wave_z

    def decay(wave_x, wave_y, wave_z):
        square = wave_x * wave_x + wave_y * wave_y + wave_z * wave_z
        return 1.0 / (1.0 + (DT * NU) * square), square

    def frame(t, first, count):
        wx, wy, wz = waves(t, first, count)
        a, square = decay(wx, wy, wz)
        flat = wx * wx + wy * wy
        inv_flat = lax.rsqrt(flat)
        inv_all = lax.rsqrt(square)
        e10, e11 = -wy * inv_flat, wx * inv_flat
        tilt = wz * inv_all
        e20, e21 = -tilt * e11, tilt * e10
        e22 = flat * inv_flat * inv_all
        return a, e10, e11, e20, e21, e22

    def z_step(t):
        half = t % 2
        for c in range(3):
            for n in range(2):
                re_h, re_l = split_value(xin[t // 2, 0, n, c])
                im_h, im_l = split_value(xin[t // 2, 1, n, c])
                top, low = n * 128, n * 128 + 64
                for ref, re, im in ((rh, re_h, im_h), (rl, re_l, im_l)):
                    ref[top : top + 64, 0:NZ] = re
                    ref[low : low + 64, 0:NZ] = im
                    ref[top : top + 64, NZ:] = im
                    ref[low : low + 64, NZ:] = -re
            dims = (((1,), (1,)), ((), ()))
            th, tl = tzh[half], tzl[half]
            high, low_part = rh[...], rl[...]
            got = lax.dot_general(th, high, dims, preferred_element_type=F32)
            got = got + lax.dot_general(tl, high, dims, preferred_element_type=F32)
            got = got + lax.dot_general(th, low_part, dims, preferred_element_type=F32)
            for s in range(SPACE):
                zbuf[t, s, c] = got[s * ROWS : (s + 1) * ROWS]
        recv[t, space] = zbuf[t, space]

    def z_send(t):
        for d in range(7):
            space_copy(t, d).start()

    def y_step(t):
        for d in range(7):
            space_arrival(t, d).wait_recv()
        for s in range(SPACE):
            for c in range(3):
                for n in range(2):
                    high, low = split_value(recv[t, s, c, :, n * 128 : (n + 1) * 128])
                    row = (c * 2 + n) * ROWS
                    lh[row : row + ROWS, s * 128 : (s + 1) * 128] = high
                    ll[row : row + ROWS, s * 128 : (s + 1) * 128] = low
        high, low = lh[...], ll[...]
        got = jnp.dot(high, tyh[...], preferred_element_type=F32)
        got = got + jnp.dot(low, tyh[...], preferred_element_type=F32)
        got = got + jnp.dot(high, tyl[...], preferred_element_type=F32)
        a, e10, e11, e20, e21, e22 = frame(t, space * 64 + (t % 2) * ROWS, ROWS)
        scale = DT * a
        for p in range(2):
            part = got[:, p * NY : (p + 1) * NY]
            pairs = []
            for n in range(2):
                g = [part[(c * 2 + n) * ROWS : (c * 2 + n + 1) * ROWS] for c in range(3)]
                pairs.append(
                    (
                        scale * (e10 * g[0] + e11 * g[1]),
                        scale * (e20 * g[0] + e21 * g[1] + e22 * g[2]),
                    )
                )
            for q in range(2):
                first = pairs[0][q]
                both = pairs[1][q] + a * first
                for k in range(2):
                    phi[t, q * 4 + p * 2 + k] = first[k * PIECE : (k + 1) * PIECE]
                    bbuf[t, q * 4 + p * 2 + k] = both[k * PIECE : (k + 1) * PIECE]
        for d in range(1, GROUP):
            forward_copy(t, d).start()
        frecv[t, mine] = bbuf[t, mine]

    def owned_decay(t):
        first = space * 64 + (t % 2) * ROWS + (mine % 2) * PIECE
        a, _ = decay(*waves(t, first, PIECE))
        return a * a

    def total_step(t):
        for d in range(1, GROUP):
            forward_copy(t, d, True).wait_recv()
        step = owned_decay(t)
        total = frecv[t, 0]
        for i in range(1, GROUP):
            total = total * step + frecv[t, i]
        tot[t] = total
        total_copy(t).start()

    def carry_step(t):
        total_copy(t).wait_recv()
        step = owned_decay(t)
        two = step * step
        four = two * two
        eight = four * four
        wrap = jnp.where(z_lo == 0, ALPHA, 1.0).astype(F32)
        carry = (wrap * zrecv[t] + ALPHA * eight * tot[t]) / (1.0 - ALPHA * eight * eight)
        for i in range(GROUP):
            cbuf[t, i] = carry
            if i < GROUP - 1:
                carry = carry * step + frecv[t, i]
        for d in range(1, GROUP):
            back_copy(t, d).start()
        crecv[t, mine] = cbuf[t, mine]

    def final_step(t):
        for d in range(1, GROUP):
            back_copy(t, d, True).wait_recv()
        for k in range(2):
            first = space * 64 + (t % 2) * ROWS + k * PIECE
            a, e10, e11, e20, e21, e22 = frame(t, first, PIECE)
            rows = slice(k * PIECE, (k + 1) * PIECE)
            for p in range(2):
                u = []
                for q in range(2):
                    j = q * 4 + p * 2 + k
                    carry = a * crecv[t, j]
                    u.append((phi[t, j] + carry, bbuf[t, j] + a * carry))
                for n in range(2):
                    u1, u2 = u[0][n], u[1][n]
                    ostage[t, p, n, 0, rows] = e10 * u1 + e20 * u2
                    ostage[t, p, n, 1, rows] = e11 * u1 + e21 * u2
                    ostage[t, p, n, 2, rows] = e22 * u2
        output_copy(t).start()

    def prologue(t, _):
        @pl.when(t % 2 == 0)
        def _():
            pltpu.make_async_copy(r_ref.at[:, :, :, t // 2], xin.at[t // 2], in_sem.at[t // 2]).wait()

        z_step(t)

        @pl.when(t == 0)
        def _():
            pl.semaphore_wait(barrier, 15)

        z_send(t)
        return 0

    tables[0].wait()
    tables[1].wait()
    lax.fori_loop(0, AHEAD, prologue, 0)
    tables[2].wait()
    tables[3].wait()

    def tick(t, _):
        @pl.when(t >= 1)
        def _():
            total_step(t - 1)

        @pl.when(t >= 2)
        def _():
            final_step(t - 2)

        y_step(t)

        @pl.when(t >= 1)
        def _():
            carry_step(t - 1)

        @pl.when(t + AHEAD < STAGES)
        def _():
            prologue(t + AHEAD, 0)

        return 0

    lax.fori_loop(0, STAGES, tick, 0)
    last = jnp.int32(STAGES - 1)
    total_step(last)
    final_step(last - 1)
    carry_step(last)
    final_step(last)

    def drain(t, _):
        for d in range(7):
            space_copy(t, d).wait_send()
        for d in range(1, GROUP):
            forward_copy(t, d).wait_send()
            back_copy(t, d).wait_send()
        total_copy(t).wait_send()
        output_copy(t).wait()
        return 0

    lax.fori_loop(0, STAGES, drain, 0)


def local(residual):
    tzh, tzl = z_tables()
    tyh, tyl = y_tables()
    any_spec = pl.BlockSpec(memory_space=pl.ANY)
    dma = pltpu.SemaphoreType.DMA
    piece = (STAGES, GROUP, PIECE, NY)
    return pl.pallas_call(
        kernel,
        out_shape=jax.ShapeDtypeStruct(residual.shape, F32),
        in_specs=[any_spec] * 5,
        out_specs=any_spec,
        scratch_shapes=[
            pltpu.VMEM((KX, 2, 2, 3, 64, NZ), F32),
            pltpu.VMEM((2, SPACE * ROWS, 2 * NZ), BF16),
            pltpu.VMEM((2, SPACE * ROWS, 2 * NZ), BF16),
            pltpu.VMEM((2 * NY, 2 * NY), BF16),
            pltpu.VMEM((2 * NY, 2 * NY), BF16),
            pltpu.VMEM((256, 2 * NZ), BF16),
            pltpu.VMEM((256, 2 * NZ), BF16),
            pltpu.VMEM((STAGES, SPACE, 3, ROWS, 256), F32),
            pltpu.VMEM((STAGES, SPACE, 3, ROWS, 256), F32),
            pltpu.VMEM((6 * ROWS, 2 * NY), BF16),
            pltpu.VMEM((6 * ROWS, 2 * NY), BF16),
            pltpu.VMEM(piece, F32),
            pltpu.VMEM(piece, F32),
            pltpu.VMEM(piece, F32),
            pltpu.VMEM((STAGES, PIECE, NY), F32),
            pltpu.VMEM((STAGES, PIECE, NY), F32),
            pltpu.VMEM(piece, F32),
            pltpu.VMEM(piece, F32),
            pltpu.VMEM((STAGES, 2, 2, 3, ROWS, NY), F32),
            dma((KX,)),
            dma((4,)),
            dma((STAGES,)),
            dma((STAGES, 8)),
            dma((STAGES, 8)),
            dma((STAGES, 8)),
            dma((STAGES, 8)),
            dma((STAGES,)),
            dma((STAGES,)),
            dma((STAGES, 8)),
            dma((STAGES, 8)),
        ],
        compiler_params=pltpu.CompilerParams(
            collective_id=0, has_side_effects=True, vmem_limit_bytes=60 * 1024 * 1024
        ),
    )(residual, tzh, tzl, tyh, tyl)


def solution(mesh):
    spec = P(None, "tm", None, None, "space", None)
    return jax.shard_map(local, mesh=mesh, in_specs=(spec,), out_specs=spec, check_vma=False)
```

```python
import math

import jax
import jax.numpy as jnp
import ml_dtypes
import numpy as np
from jax import lax
from jax.experimental import pallas as pl
from jax.experimental.pallas import tpu as pltpu
from jax.sharding import PartitionSpec as P

NY = 512
NZ = 512
TS = 32
KX = 4
ALPHA = 0.1
DT = 0.25
NU = 6e-05

MESH = pl.DeviceIdType.MESH
F32 = jnp.float32
BF16 = jnp.bfloat16

CUTS = 2
STAGES = KX * CUTS
ROWS = 64 // CUTS
TOGETHER = CUTS // 2
SPACE = 8
GROUP = 8
PIECE = ROWS // 2
AHEAD = 2
PEERS = ((0, 1), (1, 0), (3, 0), (2, 1), (1, 1), (2, 0), (3, 1))


def split_table(table):
    table = table.astype(np.float32)
    high = table.astype(ml_dtypes.bfloat16)
    low = (table - high.astype(np.float32)).astype(ml_dtypes.bfloat16)
    return high, low


def fourier(length):
    index = np.arange(length)
    angle = 2.0 * np.pi / length * (index[:, None] * index[None, :] % length)
    return np.cos(angle) / np.sqrt(length), np.sin(angle) / np.sqrt(length)


def z_tables():
    cosine, sine = fourier(NZ)
    both = np.concatenate([cosine, sine], axis=1)
    both = both.reshape(SPACE, CUTS, ROWS, 2 * NZ).transpose(1, 0, 2, 3)
    return split_table(both.reshape(2, NZ // 2, 2 * NZ))


def y_tables():
    cosine, sine = fourier(NY)
    local = NY // SPACE
    from_re = np.concatenate([cosine, -sine], axis=1).reshape(SPACE, 1, local, 2 * NY)
    from_im = np.concatenate([sine, cosine], axis=1).reshape(SPACE, 1, local, 2 * NY)
    both = np.concatenate([from_re, from_im], axis=1)
    return split_table(both.reshape(2 * NY, 2 * NY))


def split_value(value):
    high = value.astype(BF16)
    return high, (value - high.astype(F32)).astype(BF16)


def kernel(
    r_ref, tzh_ref, tzl_ref, tyh_ref, tyl_ref, out_ref,
    xin, tzh, tzl, tyh, tyl, rh, rl, zbuf, recv, lh, ll, phi, bbuf, frecv, tot, zrecv, cbuf, crecv,
    in_sem, tab_sem, zs_sem, zr_sem, fs_sem, fr_sem, es_sem, er_sem, bs_sem, br_sem,
):
    tm, space = lax.axis_index("tm"), lax.axis_index("space")
    z_lo, mine = tm // GROUP, tm % GROUP
    z_hi, y_pos = space // 4, space % 4
    partner = (1 - z_lo) * GROUP + mine

    def peer(d):
        dy, dz = PEERS[d]
        return ((z_hi + dz) % 2) * 4 + (y_pos + dy) % 4

    planes = [
        pltpu.make_async_copy(r_ref.at[:, :, :, x], xin.at[x], in_sem.at[x])
        for x in range(KX)
    ]
    tables = [
        pltpu.make_async_copy(src, dst, tab_sem.at[i])
        for i, (src, dst) in enumerate(
            ((tzh_ref, tzh), (tzl_ref, tzl), (tyh_ref, tyh), (tyl_ref, tyl))
        )
    ]
    planes[0].start()
    for table in tables:
        table.start()
    for plane in planes[1:]:
        plane.start()

    barrier = pltpu.get_barrier_semaphore()
    for d in range(7):
        pl.semaphore_signal(barrier, inc=1, device_id=(tm, peer(d)), device_id_type=MESH)
    for d in range(1, GROUP):
        other = z_lo * GROUP + (mine + d) % GROUP
        pl.semaphore_signal(barrier, inc=1, device_id=(other, space), device_id_type=MESH)
    pl.semaphore_signal(barrier, inc=1, device_id=(partner, space), device_id_type=MESH)

    def space_copy(t, d):
        return pltpu.make_async_remote_copy(
            src_ref=zbuf.at[t, peer(d)], dst_ref=recv.at[t, space],
            send_sem=zs_sem.at[t, d], recv_sem=zr_sem.at[t, space],
            device_id=(tm, peer(d)), device_id_type=MESH,
        )

    def space_arrival(t, d):
        return pltpu.make_async_remote_copy(
            src_ref=zbuf.at[t, peer(d)], dst_ref=recv.at[t, peer(d)],
            send_sem=zs_sem.at[t, d], recv_sem=zr_sem.at[t, peer(d)],
            device_id=(tm, peer(d)), device_id_type=MESH,
        )

    def group_copy(src, dst, ssem, rsem, t, d, arrival):
        other = (mine + d) % GROUP
        slot = other if arrival else mine
        return pltpu.make_async_remote_copy(
            src_ref=src.at[t, other], dst_ref=dst.at[t, slot],
            send_sem=ssem.at[t, d], recv_sem=rsem.at[t, slot],
            device_id=(z_lo * GROUP + other, space), device_id_type=MESH,
        )

    def forward_copy(t, d, arrival=False):
        return group_copy(bbuf, frecv, fs_sem, fr_sem, t, d, arrival)

    def back_copy(t, d, arrival=False):
        return group_copy(cbuf, crecv, bs_sem, br_sem, t, d, arrival)

    def total_copy(t):
        return pltpu.make_async_remote_copy(
            src_ref=tot.at[t], dst_ref=zrecv.at[t], send_sem=es_sem.at[t], recv_sem=er_sem.at[t],
            device_id=(partner, space), device_id_type=MESH,
        )

    def waves(t, first, count):
        row = lax.broadcasted_iota(jnp.int32, (count, NY), 0) + first
        col = lax.broadcasted_iota(jnp.int32, (count, NY), 1)
        wave_z = jnp.where(row < NZ // 2, row, row - NZ).astype(F32)
        wave_y = jnp.where(col < NY // 2, col, col - NY).astype(F32)
        wave_x = (t // CUTS + 1).astype(F32)
        return wave_x, wave_y, wave_z

    def decay(wave_x, wave_y, wave_z):
        square = wave_x * wave_x + wave_y * wave_y + wave_z * wave_z
        return 1.0 / (1.0 + (DT * NU) * square), square

    def frame(t, first, count):
        wx, wy, wz = waves(t, first, count)
        a, square = decay(wx, wy, wz)
        flat = wx * wx + wy * wy
        inv_flat = lax.rsqrt(flat)
        inv_all = lax.rsqrt(square)
        e10, e11 = -wy * inv_flat, wx * inv_flat
        tilt = wz * inv_all
        e20, e21 = -tilt * e11, tilt * e10
        e22 = flat * inv_flat * inv_all
        return a, e10, e11, e20, e21, e22

    def z_step(h):
        half, x = h % 2, h // 2
        for c in range(3):
            for n in range(2):
                re_h, re_l = split_value(xin[x, 0, n, c])
                im_h, im_l = split_value(xin[x, 1, n, c])
                top, low = n * 128, n * 128 + 64
                for ref, re, im in ((rh, re_h, im_h), (rl, re_l, im_l)):
                    ref[top : top + 64, 0:NZ] = re
                    ref[low : low + 64, 0:NZ] = im
                    ref[top : top + 64, NZ:] = im
                    ref[low : low + 64, NZ:] = -re
            dims = (((1,), (1,)), ((), ()))
            th, tl = tzh[half], tzl[half]
            high, low_part = rh[...], rl[...]
            got = lax.dot_general(th, high, dims, preferred_element_type=F32)
            got = got + lax.dot_general(tl, high, dims, preferred_element_type=F32)
            got = got + lax.dot_general(th, low_part, dims, preferred_element_type=F32)
            for k in range(TOGETHER):
                for s in range(SPACE):
                    row = (k * SPACE + s) * ROWS
                    zbuf[h * TOGETHER + k, s, c] = got[row : row + ROWS]
        for k in range(TOGETHER):
            recv[h * TOGETHER + k, space] = zbuf[h * TOGETHER + k, space]

    def z_send(t):
        for d in range(7):
            space_copy(t, d).start()

    def space_wait(t):
        for d in range(7):
            space_arrival(t, d).wait_recv()

    def y_step(t):
        for s in range(SPACE):
            for c in range(3):
                for n in range(2):
                    high, low = split_value(recv[t, s, c, :, n * 128 : (n + 1) * 128])
                    row = (c * 2 + n) * ROWS
                    lh[row : row + ROWS, s * 128 : (s + 1) * 128] = high
                    ll[row : row + ROWS, s * 128 : (s + 1) * 128] = low
        high, low = lh[...], ll[...]
        got = jnp.dot(high, tyh[...], preferred_element_type=F32)
        got = got + jnp.dot(low, tyh[...], preferred_element_type=F32)
        got = got + jnp.dot(high, tyl[...], preferred_element_type=F32)
        a, e10, e11, e20, e21, e22 = frame(t, space * 64 + (t % CUTS) * ROWS, ROWS)
        scale = DT * a
        for p in range(2):
            part = got[:, p * NY : (p + 1) * NY]
            pairs = []
            for n in range(2):
                g = [part[(c * 2 + n) * ROWS : (c * 2 + n + 1) * ROWS] for c in range(3)]
                pairs.append(
                    (
                        scale * (e10 * g[0] + e11 * g[1]),
                        scale * (e20 * g[0] + e21 * g[1] + e22 * g[2]),
                    )
                )
            for q in range(2):
                first = pairs[0][q]
                both = pairs[1][q] + a * first
                for k in range(2):
                    phi[t, q * 4 + p * 2 + k] = first[k * PIECE : (k + 1) * PIECE]
                    bbuf[t, q * 4 + p * 2 + k] = both[k * PIECE : (k + 1) * PIECE]
        for d in range(1, GROUP):
            forward_copy(t, d).start()
        frecv[t, mine] = bbuf[t, mine]

    def owned_decay(t):
        first = space * 64 + (t % CUTS) * ROWS + (mine % 2) * PIECE
        a, _ = decay(*waves(t, first, PIECE))
        return a * a

    def total_step(t):
        for d in range(1, GROUP):
            forward_copy(t, d, True).wait_recv()
        step = owned_decay(t)
        total = frecv[t, 0]
        for i in range(1, GROUP):
            total = total * step + frecv[t, i]
        tot[t] = total
        total_copy(t).start()

    def carry_step(t):
        total_copy(t).wait_recv()
        step = owned_decay(t)
        two = step * step
        four = two * two
        eight = four * four
        wrap = jnp.where(z_lo == 0, ALPHA, 1.0).astype(F32)
        carry = (wrap * zrecv[t] + ALPHA * eight * tot[t]) / (1.0 - ALPHA * eight * eight)
        for i in range(GROUP):
            cbuf[t, i] = carry
            if i < GROUP - 1:
                carry = carry * step + frecv[t, i]
        for d in range(1, GROUP):
            back_copy(t, d).start()
        crecv[t, mine] = cbuf[t, mine]

    def final_step(t):
        for d in range(1, GROUP):
            back_copy(t, d, True).wait_recv()
        for k in range(2):
            first = space * 64 + (t % CUTS) * ROWS + k * PIECE
            a, e10, e11, e20, e21, e22 = frame(t, first, PIECE)
            rows = pl.ds((t % CUTS) * ROWS + k * PIECE, PIECE)
            for p in range(2):
                u = []
                for q in range(2):
                    j = q * 4 + p * 2 + k
                    carry = a * crecv[t, j]
                    u.append((phi[t, j] + carry, bbuf[t, j] + a * carry))
                for n in range(2):
                    u1, u2 = u[0][n], u[1][n]
                    out_ref[p, n, 0, t // CUTS, rows] = e10 * u1 + e20 * u2
                    out_ref[p, n, 1, t // CUTS, rows] = e11 * u1 + e21 * u2
                    out_ref[p, n, 2, t // CUTS, rows] = e22 * u2

    def z_stage(t):
        @pl.when(t % CUTS == 0)
        def _():
            x = t // CUTS
            pltpu.make_async_copy(r_ref.at[:, :, :, x], xin.at[x], in_sem.at[x]).wait()

        @pl.when(t % TOGETHER == 0)
        def _():
            z_step(t // TOGETHER)

    def prologue(t, _):
        z_stage(t)

        @pl.when(t == 0)
        def _():
            pl.semaphore_wait(barrier, 15)

        z_send(t)
        return 0

    tables[0].wait()
    tables[1].wait()
    lax.fori_loop(0, AHEAD, prologue, 0)
    z_stage(jnp.int32(AHEAD))
    tables[2].wait()
    tables[3].wait()

    def tick(t, _):
        space_wait(t)

        y_step(t)

        @pl.when(t + AHEAD < STAGES)
        def _():
            z_send(t + AHEAD)

        @pl.when(t >= 1)
        def _():
            total_step(t - 1)

        @pl.when(t >= 2)
        def _():
            carry_step(t - 2)

        @pl.when(t + AHEAD + 1 < STAGES)
        def _():
            z_stage(t + AHEAD + 1)

        @pl.when(t >= 3)
        def _():
            final_step(t - 3)

        return 0

    lax.fori_loop(0, STAGES, tick, 0)
    last = jnp.int32(STAGES - 1)
    total_step(last)
    carry_step(last - 1)
    final_step(last - 2)
    carry_step(last)
    final_step(last - 1)
    final_step(last)

    def drain(t, _):
        for d in range(7):
            space_copy(t, d).wait_send()
        for d in range(1, GROUP):
            forward_copy(t, d).wait_send()
            back_copy(t, d).wait_send()
        total_copy(t).wait_send()
        return 0

    lax.fori_loop(0, STAGES, drain, 0)


def local(residual):
    tzh, tzl = z_tables()
    tyh, tyl = y_tables()
    any_spec = pl.BlockSpec(memory_space=pl.ANY)
    dma = pltpu.SemaphoreType.DMA
    piece = (STAGES, GROUP, PIECE, NY)
    return pl.pallas_call(
        kernel,
        out_shape=pltpu.VMEM(residual.shape, F32),
        in_specs=[any_spec] * 5,
        out_specs=pl.BlockSpec(memory_space=pltpu.VMEM),
        scratch_shapes=[
            pltpu.VMEM((KX, 2, 2, 3, 64, NZ), F32),
            pltpu.VMEM((2, NZ // 2, 2 * NZ), BF16),
            pltpu.VMEM((2, NZ // 2, 2 * NZ), BF16),
            pltpu.VMEM((2 * NY, 2 * NY), BF16),
            pltpu.VMEM((2 * NY, 2 * NY), BF16),
            pltpu.VMEM((256, 2 * NZ), BF16),
            pltpu.VMEM((256, 2 * NZ), BF16),
            pltpu.VMEM((STAGES, SPACE, 3, ROWS, 256), F32),
            pltpu.VMEM((STAGES, SPACE, 3, ROWS, 256), F32),
            pltpu.VMEM((6 * ROWS, 2 * NY), BF16),
            pltpu.VMEM((6 * ROWS, 2 * NY), BF16),
            pltpu.VMEM(piece, F32),
            pltpu.VMEM(piece, F32),
            pltpu.VMEM(piece, F32),
            pltpu.VMEM((STAGES, PIECE, NY), F32),
            pltpu.VMEM((STAGES, PIECE, NY), F32),
            pltpu.VMEM(piece, F32),
            pltpu.VMEM(piece, F32),
                dma((KX,)),
            dma((4,)),
            dma((STAGES, 8)),
            dma((STAGES, 8)),
            dma((STAGES, 8)),
            dma((STAGES, 8)),
            dma((STAGES,)),
            dma((STAGES,)),
            dma((STAGES, 8)),
            dma((STAGES, 8)),
        ],
        compiler_params=pltpu.CompilerParams(
            collective_id=0, has_side_effects=True, vmem_limit_bytes=48 * 1024 * 1024
        ),
    )(residual, tzh, tzl, tyh, tyl)


def solution(mesh):
    spec = P(None, "tm", None, None, "space", None)
    return jax.shard_map(local, mesh=mesh, in_specs=(spec,), out_specs=spec, check_vma=False)
```

```python
import math

import jax
import jax.numpy as jnp
import ml_dtypes
import numpy as np
from jax import lax
from jax.experimental import pallas as pl
from jax.experimental.pallas import tpu as pltpu
from jax.sharding import PartitionSpec as P

NY = 512
NZ = 512
TS = 32
KX = 4
ALPHA = 0.1
DT = 0.25
NU = 6e-05

MESH = pl.DeviceIdType.MESH
F32 = jnp.float32
BF16 = jnp.bfloat16

CUTS = 2
STAGES = KX * CUTS
ROWS = 64 // CUTS
TOGETHER = CUTS // 2
SPACE = 8
GROUP = 8
PIECE = ROWS // 2
AHEAD = 2
ORDER = (4, 3, 5, 2, 6, 1, 7)
PEERS = ((0, 1), (1, 0), (3, 0), (2, 1), (1, 1), (2, 0), (3, 1))


def split_table(table):
    table = table.astype(np.float32)
    high = table.astype(ml_dtypes.bfloat16)
    low = (table - high.astype(np.float32)).astype(ml_dtypes.bfloat16)
    return high, low


def fourier(length):
    index = np.arange(length)
    angle = 2.0 * np.pi / length * (index[:, None] * index[None, :] % length)
    return np.cos(angle) / np.sqrt(length), np.sin(angle) / np.sqrt(length)


def z_tables():
    cosine, sine = fourier(NZ)
    both = np.concatenate([cosine, sine], axis=1)
    both = both.reshape(SPACE, CUTS, ROWS, 2 * NZ).transpose(1, 0, 2, 3)
    return split_table(both.reshape(2, NZ // 2, 2 * NZ))


def y_tables():
    cosine, sine = fourier(NY)
    local = NY // SPACE
    from_re = np.concatenate([cosine, -sine], axis=1).reshape(SPACE, 1, local, 2 * NY)
    from_im = np.concatenate([sine, cosine], axis=1).reshape(SPACE, 1, local, 2 * NY)
    both = np.concatenate([from_re, from_im], axis=1)
    return split_table(both.reshape(2 * NY, 2 * NY))


def split_value(value):
    high = value.astype(BF16)
    return high, (value - high.astype(F32)).astype(BF16)


def kernel(
    r_ref, tzh_ref, tzl_ref, tyh_ref, tyl_ref, out_ref,
    xin, tzh, tzl, tyh, tyl, rh, rl, zbuf, recv, lh, ll, phi, bbuf, frecv, tot, zrecv, cbuf, crecv,
    in_sem, tab_sem, zs_sem, zr_sem, fs_sem, fr_sem, es_sem, er_sem, bs_sem, br_sem,
):
    tm, space = lax.axis_index("tm"), lax.axis_index("space")
    z_lo, mine = tm // GROUP, tm % GROUP
    z_hi, y_pos = space // 4, space % 4
    partner = (1 - z_lo) * GROUP + mine

    def peer(d):
        dy, dz = PEERS[d]
        return ((z_hi + dz) % 2) * 4 + (y_pos + dy) % 4

    planes = [
        pltpu.make_async_copy(r_ref.at[:, :, :, x], xin.at[x], in_sem.at[x])
        for x in range(KX)
    ]
    tables = [
        pltpu.make_async_copy(src, dst, tab_sem.at[i])
        for i, (src, dst) in enumerate(
            ((tzh_ref, tzh), (tzl_ref, tzl), (tyh_ref, tyh), (tyl_ref, tyl))
        )
    ]
    planes[0].start()
    for table in tables:
        table.start()
    for plane in planes[1:]:
        plane.start()

    barrier = pltpu.get_barrier_semaphore()
    for d in range(7):
        pl.semaphore_signal(barrier, inc=1, device_id=(tm, peer(d)), device_id_type=MESH)
    for d in range(1, GROUP):
        other = z_lo * GROUP + (mine + d) % GROUP
        pl.semaphore_signal(barrier, inc=1, device_id=(other, space), device_id_type=MESH)
    pl.semaphore_signal(barrier, inc=1, device_id=(partner, space), device_id_type=MESH)

    def space_copy(t, d):
        return pltpu.make_async_remote_copy(
            src_ref=zbuf.at[t, peer(d)], dst_ref=recv.at[t, space],
            send_sem=zs_sem.at[t, d], recv_sem=zr_sem.at[t, space],
            device_id=(tm, peer(d)), device_id_type=MESH,
        )

    def space_arrival(t, d):
        return pltpu.make_async_remote_copy(
            src_ref=zbuf.at[t, peer(d)], dst_ref=recv.at[t, peer(d)],
            send_sem=zs_sem.at[t, d], recv_sem=zr_sem.at[t, peer(d)],
            device_id=(tm, peer(d)), device_id_type=MESH,
        )

    def group_copy(src, dst, ssem, rsem, t, d, arrival):
        other = (mine + d) % GROUP
        slot = other if arrival else mine
        return pltpu.make_async_remote_copy(
            src_ref=src.at[t, other], dst_ref=dst.at[t, slot],
            send_sem=ssem.at[t, d], recv_sem=rsem.at[t, slot],
            device_id=(z_lo * GROUP + other, space), device_id_type=MESH,
        )

    def forward_copy(t, d, arrival=False):
        return group_copy(bbuf, frecv, fs_sem, fr_sem, t, d, arrival)

    def back_copy(t, d, arrival=False):
        return group_copy(cbuf, crecv, bs_sem, br_sem, t, d, arrival)

    def total_copy(t):
        return pltpu.make_async_remote_copy(
            src_ref=tot.at[t], dst_ref=zrecv.at[t], send_sem=es_sem.at[t], recv_sem=er_sem.at[t],
            device_id=(partner, space), device_id_type=MESH,
        )

    def waves(t, first, count):
        row = lax.broadcasted_iota(jnp.int32, (count, NY), 0) + first
        col = lax.broadcasted_iota(jnp.int32, (count, NY), 1)
        wave_z = jnp.where(row < NZ // 2, row, row - NZ).astype(F32)
        wave_y = jnp.where(col < NY // 2, col, col - NY).astype(F32)
        wave_x = (t // CUTS + 1).astype(F32)
        return wave_x, wave_y, wave_z

    def decay(wave_x, wave_y, wave_z):
        square = wave_x * wave_x + wave_y * wave_y + wave_z * wave_z
        return 1.0 / (1.0 + (DT * NU) * square), square

    def frame(t, first, count):
        wx, wy, wz = waves(t, first, count)
        a, square = decay(wx, wy, wz)
        flat = wx * wx + wy * wy
        inv_flat = lax.rsqrt(flat)
        inv_all = lax.rsqrt(square)
        e10, e11 = -wy * inv_flat, wx * inv_flat
        tilt = wz * inv_all
        e20, e21 = -tilt * e11, tilt * e10
        e22 = flat * inv_flat * inv_all
        return a, e10, e11, e20, e21, e22

    def z_step(h):
        half, x = h % 2, h // 2
        for c in range(3):
            for n in range(2):
                re_h, re_l = split_value(xin[x, 0, n, c])
                im_h, im_l = split_value(xin[x, 1, n, c])
                top, low = n * 128, n * 128 + 64
                for ref, re, im in ((rh, re_h, im_h), (rl, re_l, im_l)):
                    ref[top : top + 64, 0:NZ] = re
                    ref[low : low + 64, 0:NZ] = im
                    ref[top : top + 64, NZ:] = im
                    ref[low : low + 64, NZ:] = -re
            dims = (((1,), (1,)), ((), ()))
            th, tl = tzh[half], tzl[half]
            high, low_part = rh[...], rl[...]
            got = lax.dot_general(th, high, dims, preferred_element_type=F32)
            got = got + lax.dot_general(tl, high, dims, preferred_element_type=F32)
            got = got + lax.dot_general(th, low_part, dims, preferred_element_type=F32)
            for k in range(TOGETHER):
                for s in range(SPACE):
                    row = (k * SPACE + s) * ROWS
                    zbuf[h * TOGETHER + k, s, c] = got[row : row + ROWS]
        for k in range(TOGETHER):
            recv[h * TOGETHER + k, space] = zbuf[h * TOGETHER + k, space]

    def z_send(t):
        for d in range(7):
            space_copy(t, d).start()

    def space_wait(t):
        for d in range(7):
            space_arrival(t, d).wait_recv()

    def y_step(t):
        for s in range(SPACE):
            for c in range(3):
                for n in range(2):
                    high, low = split_value(recv[t, s, c, :, n * 128 : (n + 1) * 128])
                    row = (c * 2 + n) * ROWS
                    lh[row : row + ROWS, s * 128 : (s + 1) * 128] = high
                    ll[row : row + ROWS, s * 128 : (s + 1) * 128] = low
        high, low = lh[...], ll[...]
        got = jnp.dot(high, tyh[...], preferred_element_type=F32)
        got = got + jnp.dot(low, tyh[...], preferred_element_type=F32)
        got = got + jnp.dot(high, tyl[...], preferred_element_type=F32)
        a, e10, e11, e20, e21, e22 = frame(t, space * 64 + (t % CUTS) * ROWS, ROWS)
        scale = DT * a
        for p in range(2):
            part = got[:, p * NY : (p + 1) * NY]
            pairs = []
            for n in range(2):
                g = [part[(c * 2 + n) * ROWS : (c * 2 + n + 1) * ROWS] for c in range(3)]
                pairs.append(
                    (
                        scale * (e10 * g[0] + e11 * g[1]),
                        scale * (e20 * g[0] + e21 * g[1] + e22 * g[2]),
                    )
                )
            for q in range(2):
                first = pairs[0][q]
                both = pairs[1][q] + a * first
                for k in range(2):
                    phi[t, q * 4 + p * 2 + k] = first[k * PIECE : (k + 1) * PIECE]
                    bbuf[t, q * 4 + p * 2 + k] = both[k * PIECE : (k + 1) * PIECE]
        for d in ORDER:
            forward_copy(t, d).start()
        frecv[t, mine] = bbuf[t, mine]

    def owned_decay(t):
        first = space * 64 + (t % CUTS) * ROWS + (mine % 2) * PIECE
        a, _ = decay(*waves(t, first, PIECE))
        return a * a

    def total_step(t):
        for d in range(1, GROUP):
            forward_copy(t, d, True).wait_recv()
        step = owned_decay(t)
        total = frecv[t, 0]
        for i in range(1, GROUP):
            total = total * step + frecv[t, i]
        tot[t] = total
        total_copy(t).start()

    def carry_step(t):
        total_copy(t).wait_recv()
        step = owned_decay(t)
        two = step * step
        four = two * two
        eight = four * four
        wrap = jnp.where(z_lo == 0, ALPHA, 1.0).astype(F32)
        carry = (wrap * zrecv[t] + ALPHA * eight * tot[t]) / (1.0 - ALPHA * eight * eight)
        for i in range(GROUP):
            cbuf[t, i] = carry
            if i < GROUP - 1:
                carry = carry * step + frecv[t, i]
        for d in ORDER:
            back_copy(t, d).start()
        crecv[t, mine] = cbuf[t, mine]

    def final_step(t):
        for d in range(1, GROUP):
            back_copy(t, d, True).wait_recv()
        for k in range(2):
            first = space * 64 + (t % CUTS) * ROWS + k * PIECE
            a, e10, e11, e20, e21, e22 = frame(t, first, PIECE)
            rows = pl.ds((t % CUTS) * ROWS + k * PIECE, PIECE)
            for p in range(2):
                u = []
                for q in range(2):
                    j = q * 4 + p * 2 + k
                    carry = a * crecv[t, j]
                    u.append((phi[t, j] + carry, bbuf[t, j] + a * carry))
                for n in range(2):
                    u1, u2 = u[0][n], u[1][n]
                    out_ref[p, n, 0, t // CUTS, rows] = e10 * u1 + e20 * u2
                    out_ref[p, n, 1, t // CUTS, rows] = e11 * u1 + e21 * u2
                    out_ref[p, n, 2, t // CUTS, rows] = e22 * u2

    def z_stage(t):
        @pl.when(t % CUTS == 0)
        def _():
            x = t // CUTS
            pltpu.make_async_copy(r_ref.at[:, :, :, x], xin.at[x], in_sem.at[x]).wait()

        @pl.when(t % TOGETHER == 0)
        def _():
            z_step(t // TOGETHER)

    def prologue(t, _):
        z_stage(t)

        @pl.when(t == 0)
        def _():
            pl.semaphore_wait(barrier, 15)

        z_send(t)
        return 0

    tables[0].wait()
    tables[1].wait()
    lax.fori_loop(0, AHEAD, prologue, 0)
    z_stage(jnp.int32(AHEAD))
    tables[2].wait()
    tables[3].wait()

    def drain(t, _):
        for d in range(7):
            space_copy(t, d).wait_send()
        for d in range(1, GROUP):
            forward_copy(t, d).wait_send()
            back_copy(t, d).wait_send()
        total_copy(t).wait_send()
        return 0

    def tick(t, _):
        space_wait(t)

        y_step(t)

        @pl.when(t + AHEAD < STAGES)
        def _():
            z_send(t + AHEAD)

        @pl.when(t >= 1)
        def _():
            total_step(t - 1)

        @pl.when(t >= 2)
        def _():
            carry_step(t - 2)

        @pl.when(t + AHEAD + 1 < STAGES)
        def _():
            z_stage(t + AHEAD + 1)

        @pl.when(t >= 3)
        def _():
            final_step(t - 3)

        return 0

    lax.fori_loop(0, STAGES, tick, 0)
    last = jnp.int32(STAGES - 1)
    carry_step(last - 1)
    total_step(last)
    final_step(last - 2)
    lax.fori_loop(0, STAGES - 2, drain, 0)
    carry_step(last)
    final_step(last - 1)
    drain(last - 1, 0)
    final_step(last)

    drain(last, 0)


def local(residual):
    tzh, tzl = z_tables()
    tyh, tyl = y_tables()
    any_spec = pl.BlockSpec(memory_space=pl.ANY)
    dma = pltpu.SemaphoreType.DMA
    piece = (STAGES, GROUP, PIECE, NY)
    return pl.pallas_call(
        kernel,
        out_shape=pltpu.VMEM(residual.shape, F32),
        in_specs=[any_spec] * 5,
        out_specs=pl.BlockSpec(memory_space=pltpu.VMEM),
        scratch_shapes=[
            pltpu.VMEM((KX, 2, 2, 3, 64, NZ), F32),
            pltpu.VMEM((2, NZ // 2, 2 * NZ), BF16),
            pltpu.VMEM((2, NZ // 2, 2 * NZ), BF16),
            pltpu.VMEM((2 * NY, 2 * NY), BF16),
            pltpu.VMEM((2 * NY, 2 * NY), BF16),
            pltpu.VMEM((256, 2 * NZ), BF16),
            pltpu.VMEM((256, 2 * NZ), BF16),
            pltpu.VMEM((STAGES, SPACE, 3, ROWS, 256), F32),
            pltpu.VMEM((STAGES, SPACE, 3, ROWS, 256), F32),
            pltpu.VMEM((6 * ROWS, 2 * NY), BF16),
            pltpu.VMEM((6 * ROWS, 2 * NY), BF16),
            pltpu.VMEM(piece, F32),
            pltpu.VMEM(piece, F32),
            pltpu.VMEM(piece, F32),
            pltpu.VMEM((STAGES, PIECE, NY), F32),
            pltpu.VMEM((STAGES, PIECE, NY), F32),
            pltpu.VMEM(piece, F32),
            pltpu.VMEM(piece, F32),
                dma((KX,)),
            dma((4,)),
            dma((STAGES, 8)),
            dma((STAGES, 8)),
            dma((STAGES, 8)),
            dma((STAGES, 8)),
            dma((STAGES,)),
            dma((STAGES,)),
            dma((STAGES, 8)),
            dma((STAGES, 8)),
        ],
        compiler_params=pltpu.CompilerParams(
            collective_id=0, has_side_effects=True, vmem_limit_bytes=48 * 1024 * 1024
        ),
    )(residual, tzh, tzl, tyh, tyl)


def solution(mesh):
    spec = P(None, "tm", None, None, "space", None)
    return jax.shard_map(local, mesh=mesh, in_specs=(spec,), out_specs=spec, check_vma=False)
```
